32 devices in a mesh: img: 2 (over x), atom: 16 (over z, y, core).
Axes of the slice: x: 2, y: 2, z: 4, core: 2. Of those that a mesh axis runs over, the one named last changes fastest.
Arguments:
- density: bfloat16 [2, 9, 9, 49152], P('img', None, None, 'atom'), may hold values from -1.5 to 1.5
- energy_density: bfloat16 [2, 9, 9, 49152], P('img', None, None, 'atom'), may hold values from -1.5 to 1.5
- dham: bfloat16 [2, 3, 9, 9, 49152], P('img', None, None, None, 'atom'), may hold values from -1.5 to 1.5
- dovl: bfloat16 [2, 3, 9, 9, 49152], P('img', None, None, None, 'atom'), may hold values from -1.5 to 1.5
- pair_owner: int32 [2, 49152], P('img', 'atom'), may hold values from 0 to 511
- pair_partner: int32 [2, 49152], P('img', 'atom'), may hold values from 0 to 8191, as said below
- partner_species: int32 [2, 49152], P('img', 'atom'), may hold values from 0 to 3, as said below
- pair_count: int32 [2, 16], P('img', 'atom'), may hold values from 768 to 3072, as said below
- species: int32 [8192], P('atom'), may hold values from 0 to 3
- orbitals: int32 [4], replicated, may hold values from 1 to 9, as said below
- coords: float32 [2, 3, 8192], P('img', None, 'atom')
- reactant: float32 [3, 8192], P(None, 'atom')
- product: float32 [3, 8192], P(None, 'atom')
Outputs:
- band_force: float32 [2, 3, 8192], P('img', None, 'atom')
- tangent_force: float32 [2], P('img')
The draws below stay inside these ranges and needn't reach their ends.
Inputs may be any that keep to these rules, and one draw needn't show every extreme that they name: `pair_count`: each owner's live slots are its first ones; in every image some owner has all 3072 slots live, and every owner at least a quarter of them. partner_species[i, p] equals species[pair_partner[i, p]]. `pair_partner`: partners may be any atoms of the image; the first slot of owner o has its partner among the atoms of owner (o + 8) modulo 16 (owner o holds atoms o * 512 to o * 512 + 511). Species 0 has all 9 orbitals and the last species one.
All inputs are finite; a program needn't handle non-finite values.
Results may differ from the reference program's by a relative error of at most 0.0003.
Values sent between devices are 32-bit elements; how exact they have to be, the bound alone decides.
A program may use at most 64 MiB of HBM per device.

```python
import jax
import jax.numpy as jnp
from jax import lax

ORB = 9
SPECIES = 4
A_DEV = 512
P_DEV = 3072
IMAGES = 2
OWNERS = 16
ATOMS = 8192
PAIRS = 49152


def pair_lists(key):
    kinds = jax.random.randint(jax.random.fold_in(key, 101), (ATOMS,), 0, SPECIES).astype(jnp.int32)
    slots = jnp.arange(PAIRS, dtype=jnp.int32)
    owner_index = (slots // P_DEV).astype(jnp.int32)
    first_slot = slots % P_DEV == 0
    drawn_owner = jax.random.randint(jax.random.fold_in(key, 103), (IMAGES, PAIRS), 0, OWNERS).astype(jnp.int32)
    far_owner = jnp.mod(owner_index + OWNERS // 2, OWNERS).astype(jnp.int32)
    target = jnp.where(first_slot[None, :], far_owner[None, :], drawn_owner).astype(jnp.int32)
    within = jax.random.randint(jax.random.fold_in(key, 102), (IMAGES, PAIRS), 0, A_DEV).astype(jnp.int32)
    partners = (target * A_DEV + within).astype(jnp.int32)
    return (kinds, partners, kinds[partners])


def draw_species(key, part):
    return pair_lists(key)[0]


def draw_pair_partner(key, part):
    return pair_lists(key)[1]


def draw_partner_species(key, part):
    return pair_lists(key)[2]


def draw_pair_count(key, part):
    counts = jax.random.randint(jax.random.fold_in(key, 51), (IMAGES, OWNERS), P_DEV // 4, P_DEV + 1)
    chosen = jax.random.randint(jax.random.fold_in(key, 52), (IMAGES, 1), 0, OWNERS)
    owners_index = jnp.arange(OWNERS, dtype=jnp.int32)[None, :]
    return jnp.where(owners_index == chosen, P_DEV, counts).astype(jnp.int32)


def draw_orbitals(key, part):
    middle = jax.random.randint(jax.random.fold_in(key, 61), (SPECIES - 2,), 1, ORB + 1)
    return jnp.concatenate([jnp.full((1,), ORB), middle, jnp.ones((1,))]).astype(jnp.int32)


def band_point(key, index):
    base = 4.0 * jax.random.normal(jax.random.fold_in(key, 31), (3, ATOMS), jnp.float32)
    place = jnp.arange(ATOMS, dtype=jnp.float32) / max(ATOMS - 1, 1)
    image_key = jax.random.fold_in(jax.random.fold_in(key, 37), index)
    image_scale = jnp.exp(jax.random.uniform(image_key, (), jnp.float32, -0.7, 0.7))
    noise_key = jax.random.fold_in(jax.random.fold_in(key, 41), index)
    rise = 3.0 ** (0.5 * place)
    noise = jax.random.normal(noise_key, (3, ATOMS), jnp.float32)
    return base + 0.3 * image_scale * rise[None, :] * noise


def draw_coords(key, part):
    return jnp.stack([band_point(key, index) for index in range(IMAGES)], axis=0)


def draw_reactant(key, part):
    return band_point(key, 1000)


def draw_product(key, part):
    return band_point(key, 1001)


def touch_ends(values, stream_key, low, high):
    spot = [jax.random.randint(jax.random.fold_in(stream_key, axis), (), 0, length) for axis, length in enumerate(values.shape)]
    main_axis = values.shape.index(max(values.shape))
    beside = spot[:main_axis] + [(spot[main_axis] + 1) % values.shape[main_axis]] + spot[main_axis + 1:]
    return values.at[tuple(spot)].set(low).at[tuple(beside)].set(high)


def block_scale(own_key, extent, split, least, top_value):
    def one(axis_at, blocks):
        draws = jax.random.uniform(jax.random.fold_in(jax.random.fold_in(own_key, 6), axis_at), (blocks,), jnp.float32, least / len(split), top_value / len(split))
        return jnp.repeat(jnp.exp(draws), extent[axis_at] // blocks).reshape((-1,) + (1,) * (len(extent) - axis_at - 1))

    loudness = one(*split[0])
    for cut in split[1:]:
        loudness = loudness * one(*cut)
    return loudness


def normal_values(rng, extent, width, reach, pieces=(), kind=jnp.bfloat16):
    gain = block_scale(rng, extent, pieces, -0.22, 0.18) if pieces else 1.0
    drawn = jax.random.normal(rng, extent, jnp.float32) * width * gain
    return jnp.minimum(jnp.maximum(drawn, -reach), reach).astype(kind)


def setup_inputs(seed: int = 0) -> dict:
    keys = jax.random.split(jax.random.key(seed), 14)
    return {
        "density": normal_values(keys[0], (IMAGES, ORB, ORB, PAIRS), 0.25, 1.5, ((0, 2), (3, 16))),
        "energy_density": normal_values(keys[1], (IMAGES, ORB, ORB, PAIRS), 0.25, 1.5, ((0, 2), (3, 16))),
        "dham": normal_values(keys[2], (IMAGES, 3, ORB, ORB, PAIRS), 0.25, 1.5, ((0, 2), (4, 16))),
        "dovl": normal_values(keys[3], (IMAGES, 3, ORB, ORB, PAIRS), 0.25, 1.5, ((0, 2), (4, 16))),
        "pair_owner": touch_ends(jax.random.randint(keys[4], (IMAGES, PAIRS), 0, A_DEV), jax.random.fold_in(keys[4], 1), 0, A_DEV - 1).astype(jnp.int32),
        "pair_partner": draw_pair_partner(jax.random.fold_in(keys[13], 71), 0),
        "partner_species": draw_partner_species(jax.random.fold_in(keys[13], 71), 0),
        "pair_count": draw_pair_count(jax.random.fold_in(keys[13], 71), 0),
        "species": draw_species(jax.random.fold_in(keys[13], 71), 0),
        "orbitals": draw_orbitals(jax.random.fold_in(keys[13], 71), 0),
        "coords": draw_coords(jax.random.fold_in(keys[13], 71), 0),
        "reactant": draw_reactant(jax.random.fold_in(keys[13], 71), 0),
        "product": draw_product(jax.random.fold_in(keys[13], 71), 0),
    }


spring_const = 1.0
tangent_eps = 1e-06

def image_forces(items, species, orbitals):
    dens, energy, dham_img, dovl_img, owner, partner, partner_kind, count = items
    slots = jnp.arange(PAIRS, dtype=jnp.int32)
    device = (slots // P_DEV).astype(jnp.int32)
    live = slots % P_DEV < count[device]
    owner_atom = (device * A_DEV + owner).astype(jnp.int32)
    own_orbitals = orbitals[species[owner_atom]]
    partner_orbitals = orbitals[partner_kind]
    levels = jnp.arange(ORB, dtype=jnp.int32)
    row_ok = (levels[:, None] < own_orbitals[None, :]) & live[None, :]
    col_ok = levels[:, None] < partner_orbitals[None, :]
    mask = (row_ok[:, None, :] & col_ok[None, :, :]).astype(jnp.bfloat16)
    masked_density = dens * mask
    masked_energy = energy * mask
    term_ham = jnp.einsum('abp,cabp->cp', masked_density.astype(jnp.float32), dham_img.astype(jnp.float32))
    term_ovl = jnp.einsum('abp,cabp->cp', masked_energy.astype(jnp.float32), dovl_img.astype(jnp.float32))
    pair_force = -2.0 * (term_ham - term_ovl)
    total = jnp.zeros((3, ATOMS), jnp.float32)
    total = total.at[:, owner_atom].add(pair_force)
    total = total.at[:, partner].add(-pair_force)
    return total

def reference(density, energy_density, dham, dovl, pair_owner, pair_partner, partner_species, pair_count, species, orbitals, coords, reactant, product):
    items = (density, energy_density, dham, dovl, pair_owner, pair_partner, partner_species, pair_count)
    force = lax.map(lambda entry: image_forces(entry, species, orbitals), items)
    prior = jnp.concatenate([reactant[None], coords[:-1]], axis=0)
    later = jnp.concatenate([coords[1:], product[None]], axis=0)
    tangent = later - prior
    ahead = lax.optimization_barrier(jnp.sum((later - coords) ** 2, axis=(1, 2)))
    behind = lax.optimization_barrier(jnp.sum((coords - prior) ** 2, axis=(1, 2)))
    length = lax.optimization_barrier(jnp.sum(tangent * tangent, axis=(1, 2)))
    unit = tangent / jnp.sqrt(length + tangent_eps)[:, None, None]
    tangent_force = lax.optimization_barrier(jnp.sum(force * unit, axis=(1, 2)))
    spring = spring_const * (jnp.sqrt(ahead) - jnp.sqrt(behind))
    band_force = force - tangent_force[:, None, None] * unit + spring[:, None, None] * unit
    return (band_force, tangent_force)
```

```python
import functools

import jax
import jax.numpy as jnp
from jax import lax
from jax.experimental import pallas as pl
from jax.experimental.pallas import tpu as pltpu
from jax.sharding import PartitionSpec as P

MESH = pl.DeviceIdType.MESH
spring_const = 1.0
tangent_eps = 1e-06
WIDE = 256
LINES = 4


def step_kernel(
    n_img,
    n_atom,
    chunk,
    density,
    energy,
    dham,
    dovl,
    owner,
    partner,
    partner_species,
    count,
    species,
    orbitals,
    coords,
    reactant,
    product,
    band_out,
    tangent_out,
    dens_v,
    ener_v,
    dham_v,
    dovl_v,
    dens_f,
    ener_f,
    owner_v,
    partner_v,
    kind_v,
    count_s,
    species_v,
    orbitals_s,
    coords_v,
    ends_v,
    current_t,
    before_t,
    after_t,
    tan_all,
    part_all,
    recv_all,
    block_sem,
    small_sem,
    img_send,
    img_recv,
    tan_send,
    tan_recv,
    force_send,
    force_recv,
):
    f32, bf16, i32 = jnp.float32, jnp.bfloat16, jnp.int32
    img, me = lax.axis_index("img"), lax.axis_index("atom")
    n_slots = owner.shape[1]
    n_orb = density.shape[1]
    n_comp = dham.shape[3]
    n_kinds = orbitals.shape[0]
    rows_own = species.shape[0] // WIDE
    tile = rows_own * LINES
    n_chunks = n_slots // chunk

    smalls = [
        (owner, owner_v),
        (partner, partner_v),
        (partner_species, kind_v),
        (count, count_s),
        (species, species_v),
        (orbitals, orbitals_s),
        (coords, coords_v),
    ]
    small_copies = [
        pltpu.make_async_copy(src, dst, small_sem.at[i]) for i, (src, dst) in enumerate(smalls)
    ]
    for copy in small_copies:
        copy.start()
    ends = (
        pltpu.make_async_copy(reactant, ends_v.at[0], small_sem.at[len(smalls)]),
        pltpu.make_async_copy(product, ends_v.at[1], small_sem.at[len(smalls) + 1]),
    )
    first, last = img == 0, img == n_img - 1
    pl.when(first)(ends[0].start)
    pl.when(last)(ends[1].start)
    block_copies = []
    for k in range(n_chunks):
        cols = pl.ds(k * chunk, chunk)
        pairs = (
            (density.at[0, :, :, cols], dens_v.at[:, :, cols]),
            (energy.at[0, :, :, cols], ener_v.at[:, :, cols]),
            (dham.at[0, :, :, :, cols], dham_v.at[:, :, :, cols]),
            (dovl.at[0, :, :, :, cols], dovl_v.at[:, :, :, cols]),
        )
        block_copies.append(
            [pltpu.make_async_copy(s, d, block_sem.at[k, j]) for j, (s, d) in enumerate(pairs)]
        )
    for group in block_copies:
        for copy in group:
            copy.start()

    barrier = pltpu.get_barrier_semaphore()
    for s in range(1, n_atom):
        pl.semaphore_signal(
            barrier, inc=1, device_id={"atom": lax.rem(me + s, n_atom)}, device_id_type=MESH
        )

    @pl.when(img > 0)
    def _():
        pl.semaphore_signal(barrier, inc=1, device_id={"img": img - 1}, device_id_type=MESH)

    @pl.when(img < n_img - 1)
    def _():
        pl.semaphore_signal(barrier, inc=1, device_id={"img": img + 1}, device_id_type=MESH)

    for copy in small_copies:
        copy.wait()

    kinds_own = species_v[...].reshape(1, species.shape[0])
    table = jnp.zeros(kinds_own.shape, f32)
    for k in range(n_kinds):
        table = jnp.where(kinds_own == k, orbitals_s[k].astype(f32), table)
    table = jnp.concatenate(
        [table[:, h * WIDE : (h + 1) * WIDE] for h in range(rows_own)]
        + [jnp.zeros((16 - rows_own, WIDE), f32)],
        axis=0,
    ).astype(bf16)
    n_rows = n_atom * tile
    total = jnp.zeros((2 * n_rows, WIDE), f32)
    total_own = jnp.zeros((2 * tile, WIDE), f32)
    shift = WIDE.bit_length() - 1

    def onehot(low):
        return jnp.where(lax.broadcasted_iota(i32, (WIDE, chunk), 0) == low, 1.0, 0.0).astype(bf16)

    def work(k, total, total_own):
        cols = pl.ds(k * chunk, chunk)
        own = owner_v[:, cols]
        part = partner_v[:, cols]
        kind = kind_v[:, cols]
        own_hot = onehot(own & (WIDE - 1))
        part_hot = onehot(part & (WIDE - 1))
        own_row = own >> shift
        part_row = part >> shift
        picked = jnp.dot(table, own_hot, preferred_element_type=f32)
        own_orb = jnp.zeros((1, chunk), f32)
        for h in range(rows_own):
            own_orb = jnp.where(own_row == h, picked[h : h + 1], own_orb)
        part_orb = jnp.zeros((1, chunk), f32)
        for j in range(n_kinds):
            part_orb = jnp.where(kind == j, orbitals_s[j].astype(f32), part_orb)
        slot = lax.broadcasted_iota(i32, (1, chunk), 1) + k * chunk
        own_orb = jnp.where(slot < count_s[0, 0], own_orb, 0.0)
        level = lax.broadcasted_iota(i32, (n_orb, chunk), 0).astype(f32)
        for copy in block_copies[k]:
            copy.wait()
        for a in range(n_orb):
            bound = jnp.where(own_orb > a, part_orb, 0.0)
            mask = level < bound
            row = pl.ds(a * 16, n_orb)
            dens_f[row, :] = jnp.where(mask, dens_v[a, :, cols].astype(f32), 0.0)
            ener_f[row, :] = jnp.where(mask, ener_v[a, :, cols].astype(f32), 0.0)
        acc = [jnp.zeros((n_comp, chunk), f32) for _ in range(2)]
        for a in range(n_orb):
            for b in range(n_orb):
                row = pl.ds(a * 16 + b, 1)
                acc[0] = acc[0] + dens_f[row, :] * dham_v[a, b, :, cols].astype(f32)
                acc[1] = acc[1] + ener_f[row, :] * dovl_v[a, b, :, cols].astype(f32)
        force = -2.0 * (acc[0] - acc[1])
        line = lax.broadcasted_iota(i32, (tile, chunk), 0)
        lines = jnp.zeros((tile, chunk), f32)
        for c in range(n_comp):
            lines = jnp.where(line % LINES == c, force[c : c + 1], lines)
        upper = lines.astype(bf16).astype(f32)
        lower = lines - upper
        on_own = line // LINES == own_row
        lhs_own = jnp.concatenate(
            [jnp.where(on_own, upper, 0.0), jnp.where(on_own, lower, 0.0)], axis=0
        ).astype(bf16)
        pieces = []
        for value in (upper, lower):
            for d in range(n_atom):
                pieces.append(jnp.where(line // LINES + d * rows_own == part_row, value, 0.0))
        lhs = jnp.concatenate(pieces, axis=0).astype(bf16)
        dims = (((1,), (1,)), ((), ()))
        total = total + lax.dot_general(lhs, part_hot, dims, preferred_element_type=f32)
        total_own = total_own + lax.dot_general(lhs_own, own_hot, dims, preferred_element_type=f32)
        return total, total_own

    def to_next():
        return pltpu.make_async_remote_copy(
            src_ref=current_t,
            dst_ref=before_t,
            send_sem=img_send.at[0],
            recv_sem=img_recv.at[0],
            device_id={"img": img + 1},
            device_id_type=MESH,
        )

    def to_previous():
        return pltpu.make_async_remote_copy(
            src_ref=current_t,
            dst_ref=after_t,
            send_sem=img_send.at[1],
            recv_sem=img_recv.at[1],
            device_id={"img": img - 1},
            device_id_type=MESH,
        )

    def to_tile(ref, get):
        ref[...] = jnp.zeros_like(ref)
        for h in range(rows_own):
            for c in range(n_comp):
                row = h * LINES + c
                ref[row : row + 1, :] = get(c)[:, h * WIDE : (h + 1) * WIDE]

    def target(s):
        return lax.rem(me + s, n_atom)

    def tangent_copy(s):
        return pltpu.make_async_remote_copy(
            src_ref=tan_all.at[me],
            dst_ref=tan_all.at[me],
            send_sem=tan_send.at[s],
            recv_sem=tan_recv.at[me],
            device_id={"atom": target(s)},
            device_id_type=MESH,
        )

    def tangent_arrival(s):
        other = target(s)
        return pltpu.make_async_remote_copy(
            src_ref=tan_all.at[other],
            dst_ref=tan_all.at[other],
            send_sem=tan_send.at[s],
            recv_sem=tan_recv.at[other],
            device_id={"atom": other},
            device_id_type=MESH,
        )

    def force_copy(s):
        other = target(s)
        return pltpu.make_async_remote_copy(
            src_ref=part_all.at[other],
            dst_ref=recv_all.at[me],
            send_sem=force_send.at[s],
            recv_sem=force_recv.at[me],
            device_id={"atom": other},
            device_id_type=MESH,
        )

    def force_arrival(s):
        other = target(s)
        return pltpu.make_async_remote_copy(
            src_ref=part_all.at[other],
            dst_ref=recv_all.at[other],
            send_sem=force_send.at[s],
            recv_sem=force_recv.at[other],
            device_id={"atom": other},
            device_id_type=MESH,
        )

    tile_line = lax.broadcasted_iota(i32, (tile, WIDE), 0)
    greeted = (n_atom - 1) + jnp.where(img > 0, 1, 0) + jnp.where(img < n_img - 1, 1, 0)

    def send_coords():
        to_tile(current_t, lambda c: coords_v[c])
        pl.semaphore_wait(barrier, greeted)
        pl.when(img < n_img - 1)(lambda: to_next().start())
        pl.when(img > 0)(lambda: to_previous().start())

    def send_tangent():
        @pl.when(first)
        def _():
            ends[0].wait()
            to_tile(before_t, lambda c: ends_v[0, c : c + 1])

        @pl.when(last)
        def _():
            ends[1].wait()
            to_tile(after_t, lambda c: ends_v[1, c : c + 1])

        pl.when(img > 0)(lambda: to_next().wait_recv())
        pl.when(img < n_img - 1)(lambda: to_previous().wait_recv())
        current, before, after = current_t[...], before_t[...], after_t[...]
        ahead = jnp.sum((after - current) ** 2, axis=0, keepdims=True)
        behind = jnp.sum((current - before) ** 2, axis=0, keepdims=True)
        mine = after - before
        mine = jnp.where(tile_line == LINES - 1, ahead, mine)
        mine = jnp.where(tile_line == 2 * LINES - 1, behind, mine)
        tan_all[me] = mine
        for s in range(1, n_atom):
            tangent_copy(s).start()

    early = min(1, n_chunks - 1)
    middle = min(3, n_chunks - 1)
    for k in range(n_chunks):
        if k == early:
            send_coords()
        if k == middle:
            send_tangent()
        total, total_own = work(k, total, total_own)

    for s in range(1, n_atom):
        tangent_arrival(s).wait_recv()
    partner_sum = total[:n_rows] + total[n_rows:]
    own_sum = total_own[:tile] + total_own[tile:]
    plain = tile_line % LINES < n_comp
    parts, dot = [], jnp.zeros((tile, WIDE), f32)
    square = jnp.zeros((tile, WIDE), f32)
    sums = jnp.zeros((tile, WIDE), f32)
    for d in range(n_atom):
        value = jnp.where(me == d, own_sum, 0.0) - partner_sum[d * tile : (d + 1) * tile]
        other = tan_all[d]
        tangent = jnp.where(plain, other, 0.0)
        dot = dot + value * tangent
        square = square + tangent * tangent
        sums = sums + other
        parts.append(value)
    dot = jnp.sum(dot, axis=0, keepdims=True)
    for d in range(n_atom):
        part_all[d] = jnp.where(tile_line == LINES - 1, dot, parts[d])
    for s in range(1, n_atom):
        force_copy(s).start()
    recv_all[me] = part_all[me]
    length = jnp.sum(square, keepdims=True)
    ahead = jnp.sum(sums[LINES - 1 : LINES], keepdims=True)
    behind = jnp.sum(sums[2 * LINES - 1 : 2 * LINES], keepdims=True)
    inverse = 1.0 / jnp.sqrt(length + tangent_eps)
    spring = spring_const * (jnp.sqrt(ahead) - jnp.sqrt(behind))
    for s in range(1, n_atom):
        force_arrival(s).wait_recv()
    summed = recv_all[0]
    for d in range(1, n_atom):
        summed = summed + recv_all[d]
    along = jnp.sum(summed[LINES - 1 : LINES], keepdims=True) * inverse
    band = summed + ((spring - along) * inverse) * tan_all[me]
    for h in range(rows_own):
        for c in range(n_comp):
            row = h * LINES + c
            band_out[c, :, h * WIDE : (h + 1) * WIDE] = band[row : row + 1]
    tangent_out[...] = along
    pl.when(img < n_img - 1)(lambda: to_next().wait_send())
    pl.when(img > 0)(lambda: to_previous().wait_send())
    for s in range(1, n_atom):
        tangent_copy(s).wait_send()
        force_copy(s).wait_send()


def solution(mesh):
    n_img, n_atom = mesh.shape["img"], mesh.shape["atom"]

    def local(density, energy, dham, dovl, owner, partner, kind, count, species, *rest):
        orbitals, coords, reactant, product = rest
        dham, dovl = (jnp.transpose(x, (0, 2, 3, 1, 4)) for x in (dham, dovl))
        coords = jnp.transpose(coords, (1, 0, 2))
        args = (density, energy, dham, dovl, owner, partner, kind, count, species)
        args += (orbitals, coords, reactant, product)
        n_slots, n_orb = owner.shape[1], density.shape[1]
        chunk = next(c for c in (512, 256, 128) if n_slots % c == 0)
        tile = species.shape[0] // WIDE * LINES
        tiles = (n_atom, tile, WIDE)
        dma = pltpu.SemaphoreType.DMA
        band, along = pl.pallas_call(
            functools.partial(step_kernel, n_img, n_atom, chunk),
            out_shape=(
                jax.ShapeDtypeStruct(coords.shape, jnp.float32),
                jax.ShapeDtypeStruct((1, 1), jnp.float32),
            ),
            in_specs=[pl.BlockSpec(memory_space=pltpu.HBM)] * len(args),
            out_specs=(
                pl.BlockSpec(memory_space=pltpu.VMEM),
                pl.BlockSpec(memory_space=pltpu.VMEM),
            ),
            scratch_shapes=[
                pltpu.VMEM(density.shape[1:], jnp.bfloat16),
                pltpu.VMEM(density.shape[1:], jnp.bfloat16),
                pltpu.VMEM(dham.shape[1:], jnp.bfloat16),
                pltpu.VMEM(dham.shape[1:], jnp.bfloat16),
                pltpu.VMEM((n_orb * 16, chunk), jnp.float32),
                pltpu.VMEM((n_orb * 16, chunk), jnp.float32),
                pltpu.VMEM(owner.shape, jnp.int32),
                pltpu.VMEM(owner.shape, jnp.int32),
                pltpu.VMEM(owner.shape, jnp.int32),
                pltpu.SMEM(count.shape, jnp.int32),
                pltpu.VMEM(species.shape, jnp.int32),
                pltpu.SMEM(orbitals.shape, jnp.int32),
                pltpu.VMEM(coords.shape, jnp.float32),
                pltpu.VMEM((2,) + reactant.shape, jnp.float32),
                pltpu.VMEM(tiles[1:], jnp.float32),
                pltpu.VMEM(tiles[1:], jnp.float32),
                pltpu.VMEM(tiles[1:], jnp.float32),
                pltpu.VMEM(tiles, jnp.float32),
                pltpu.VMEM(tiles, jnp.float32),
                pltpu.VMEM(tiles, jnp.float32),
                dma((n_slots // chunk, 4)),
                dma((9,)),
                dma((2,)),
                dma((2,)),
                dma((n_atom,)),
                dma((n_atom,)),
                dma((n_atom,)),
                dma((n_atom,)),
            ],
            compiler_params=pltpu.CompilerParams(
                collective_id=0, has_side_effects=True, vmem_limit_bytes=63 * 1024 * 1024
            ),
        )(*args)
        return jnp.transpose(band, (1, 0, 2)), jnp.reshape(along, (1,))

    return jax.shard_map(
        local,
        mesh=mesh,
        in_specs=(
            P("img", None, None, "atom"),
            P("img", None, None, "atom"),
            P("img", None, None, None, "atom"),
            P("img", None, None, None, "atom"),
            P("img", "atom"),
            P("img", "atom"),
            P("img", "atom"),
            P("img", "atom"),
            P("atom"),
            P(),
            P("img", None, "atom"),
            P(None, "atom"),
            P(None, "atom"),
        ),
        out_specs=(P("img", None, "atom"), P("img")),
        check_vma=False,
    )
```

```python
import functools

import jax
import jax.numpy as jnp
from jax import lax
from jax.experimental import pallas as pl
from jax.experimental.pallas import tpu as pltpu
from jax.sharding import PartitionSpec as P

MESH = pl.DeviceIdType.MESH
spring_const = 1.0
tangent_eps = 1e-06
WIDE = 256
LINES = 4


def step_kernel(
    n_img,
    n_atom,
    chunk,
    density,
    energy,
    dham,
    dovl,
    owner,
    partner,
    partner_species,
    count,
    species,
    orbitals,
    coords,
    reactant,
    product,
    force_out,
    pull_out,
    tangent_out,
    dens_v,
    ener_v,
    dham_v,
    dovl_v,
    dens_f,
    ener_f,
    own_hot,
    part_hot,
    orb_v,
    total,
    total_own,
    owner_v,
    partner_v,
    kind_v,
    count_s,
    species_v,
    orbitals_s,
    coords_v,
    ends_v,
    current_t,
    before_t,
    after_t,
    tan_all,
    part_all,
    recv_all,
    block_sem,
    small_sem,
    img_send,
    img_recv,
    tan_send,
    tan_recv,
    force_send,
    force_recv,
):
    f32, bf16, i32 = jnp.float32, jnp.bfloat16, jnp.int32
    img, me = lax.axis_index("img"), lax.axis_index("atom")
    n_slots = owner.shape[1]
    n_orb = density.shape[1]
    n_comp = dham.shape[3]
    n_kinds = orbitals.shape[0]
    rows_own = species.shape[0] // WIDE
    tile = rows_own * LINES
    n_chunks = n_slots // chunk

    smalls = [
        (owner, owner_v),
        (partner, partner_v),
        (partner_species, kind_v),
        (count, count_s),
        (species, species_v),
        (orbitals, orbitals_s),
        (coords, coords_v),
    ]
    small_copies = [
        pltpu.make_async_copy(src, dst, small_sem.at[i]) for i, (src, dst) in enumerate(smalls)
    ]
    for copy in small_copies:
        copy.start()
    ends = (
        pltpu.make_async_copy(reactant, ends_v.at[0], small_sem.at[len(smalls)]),
        pltpu.make_async_copy(product, ends_v.at[1], small_sem.at[len(smalls) + 1]),
    )
    first, last = img == 0, img == n_img - 1
    pl.when(first)(ends[0].start)
    pl.when(last)(ends[1].start)

    def block_pairs(k):
        cols = pl.ds(k * chunk if isinstance(k, int) else pl.multiple_of(k * chunk, chunk), chunk)
        return (
            (density.at[0, :, :, cols], dens_v.at[:, :, cols]),
            (energy.at[0, :, :, cols], ener_v.at[:, :, cols]),
            (dham.at[0, :, :, :, cols], dham_v.at[:, :, :, cols]),
            (dovl.at[0, :, :, :, cols], dovl_v.at[:, :, :, cols]),
        )

    def fetch(k, carry):
        for j, (src, dst) in enumerate(block_pairs(k)):
            pltpu.make_async_copy(src, dst, block_sem.at[k, j]).start()
        return carry

    lax.fori_loop(0, n_chunks, fetch, 0)

    barrier = pltpu.get_barrier_semaphore()
    for s in range(1, n_atom):
        pl.semaphore_signal(
            barrier, inc=1, device_id={"atom": lax.rem(me + s, n_atom)}, device_id_type=MESH
        )

    @pl.when(img > 0)
    def _():
        pl.semaphore_signal(barrier, inc=1, device_id={"img": img - 1}, device_id_type=MESH)

    @pl.when(img < n_img - 1)
    def _():
        pl.semaphore_signal(barrier, inc=1, device_id={"img": img + 1}, device_id_type=MESH)

    for copy in small_copies:
        copy.wait()

    kinds_own = species_v[...].reshape(1, species.shape[0])
    table = jnp.zeros(kinds_own.shape, f32)
    for k in range(n_kinds):
        table = jnp.where(kinds_own == k, orbitals_s[k].astype(f32), table)
    table = jnp.concatenate(
        [table[:, h * WIDE : (h + 1) * WIDE] for h in range(rows_own)]
        + [jnp.zeros((16 - rows_own, WIDE), f32)],
        axis=0,
    ).astype(bf16)
    n_rows = n_atom * tile
    shift = WIDE.bit_length() - 1
    pack = 16
    dims = (((1,), (1,)), ((), ()))
    zero = jnp.zeros((), bf16)
    pack_line = lax.broadcasted_iota(i32, (pack, chunk), 0)
    pack_row = pack_line.astype(f32).astype(bf16)
    atom_row = (pack_line // LINES).astype(f32).astype(bf16)
    own_atom_row = (pack_line % tile // LINES).astype(f32).astype(bf16)
    level = lax.broadcasted_iota(i32, (n_orb, chunk), 0).astype(f32).astype(bf16)

    def columns(k):
        return pl.ds(pl.multiple_of(k * chunk, chunk), chunk)

    def small(values):
        return values.astype(f32).astype(bf16)

    def prepare(k, carry):
        cols = columns(k)
        own = owner_v[:, cols]
        part = partner_v[:, cols]
        kind = kind_v[:, cols]
        for index, hot in ((own, own_hot), (part, part_hot)):
            low = jnp.broadcast_to(small(index & (WIDE - 1)), (pack, chunk))
            for g in range(WIDE // pack):
                match = pack_row == low - jnp.asarray(g * pack, bf16)
                hot[g * pack : (g + 1) * pack, cols] = jnp.where(match, zero + 1, zero)
        own_row = own >> shift
        picked = jnp.dot(table, own_hot[:, cols], preferred_element_type=f32)
        own_orb = jnp.zeros((1, chunk), f32)
        for h in range(rows_own):
            own_orb = jnp.where(own_row == h, picked[h : h + 1], own_orb)
        part_orb = jnp.zeros((1, chunk), f32)
        for j in range(n_kinds):
            part_orb = jnp.where(kind == j, orbitals_s[j].astype(f32), part_orb)
        slot = lax.broadcasted_iota(i32, (1, chunk), 1) + k * chunk
        orb_v[0:1, cols] = jnp.where(slot < count_s[0, 0], own_orb, 0.0)
        orb_v[1:2, cols] = part_orb
        return carry

    def work(k, carry):
        pl.when(k == middle)(send_tangent)
        cols = columns(k)
        own_orb, part_orb = orb_v[0:1, cols], orb_v[1:2, cols]
        for j, (src, dst) in enumerate(block_pairs(k)):
            pltpu.make_async_copy(src, dst, block_sem.at[k, j]).wait()
        for a in range(n_orb):
            bound = jnp.where(own_orb > a, part_orb, 0.0).astype(bf16)
            mask = level < bound
            row = pl.ds(a * 16, n_orb)
            dens_f[row, :] = jnp.where(mask, dens_v[a, :, cols], zero).astype(f32)
            ener_f[row, :] = jnp.where(mask, ener_v[a, :, cols], zero).astype(f32)
        acc = [jnp.zeros((n_comp, chunk), f32) for _ in range(2)]
        for a in range(n_orb):
            for b in range(n_orb):
                row = pl.ds(a * 16 + b, 1)
                acc[0] = acc[0] + dens_f[row, :] * dham_v[a, b, :, cols].astype(f32)
                acc[1] = acc[1] + ener_f[row, :] * dovl_v[a, b, :, cols].astype(f32)
        force = -2.0 * (acc[0] - acc[1])
        line = lax.broadcasted_iota(i32, (tile, chunk), 0)
        lines = jnp.zeros((tile, chunk), f32)
        for c in range(n_comp):
            lines = jnp.where(line % LINES == c, force[c : c + 1], lines)
        upper = lines.astype(bf16).astype(f32)
        lower = lines - upper
        own_row = jnp.broadcast_to(small(owner_v[:, cols] >> shift), (pack, chunk))
        part_row = jnp.broadcast_to(small(partner_v[:, cols] >> shift), (pack, chunk))
        both = jnp.concatenate([upper, lower], axis=0).astype(bf16)
        lhs_own = jnp.where(own_atom_row == own_row, both, zero)
        twice = [jnp.concatenate([v] * (pack // tile), axis=0).astype(bf16) for v in (upper, lower)]
        uppers, lowers = [], []
        for g in range(n_rows // pack):
            match = atom_row == part_row - jnp.asarray(g * (pack // LINES), bf16)
            uppers.append(jnp.where(match, twice[0], zero))
            lowers.append(jnp.where(match, twice[1], zero))
        lhs = jnp.concatenate(uppers + lowers, axis=0)
        total[...] += lax.dot_general(lhs, part_hot[:, cols], dims, preferred_element_type=f32)
        total_own[...] += lax.dot_general(
            lhs_own, own_hot[:, cols], dims, preferred_element_type=f32
        )
        return carry

    def to_next():
        return pltpu.make_async_remote_copy(
            src_ref=current_t,
            dst_ref=before_t,
            send_sem=img_send.at[0],
            recv_sem=img_recv.at[0],
            device_id={"img": img + 1},
            device_id_type=MESH,
        )

    def to_previous():
        return pltpu.make_async_remote_copy(
            src_ref=current_t,
            dst_ref=after_t,
            send_sem=img_send.at[1],
            recv_sem=img_recv.at[1],
            device_id={"img": img - 1},
            device_id_type=MESH,
        )

    def to_tile(ref, get):
        ref[...] = jnp.zeros_like(ref)
        for h in range(rows_own):
            for c in range(n_comp):
                row = h * LINES + c
                ref[row : row + 1, :] = get(c)[:, h * WIDE : (h + 1) * WIDE]

    def target(s):
        return lax.rem(me + s, n_atom)

    def tangent_copy(s):
        return pltpu.make_async_remote_copy(
            src_ref=tan_all.at[me],
            dst_ref=tan_all.at[me],
            send_sem=tan_send.at[s],
            recv_sem=tan_recv.at[me],
            device_id={"atom": target(s)},
            device_id_type=MESH,
        )

    def tangent_arrival(s):
        other = target(s)
        return pltpu.make_async_remote_copy(
            src_ref=tan_all.at[other],
            dst_ref=tan_all.at[other],
            send_sem=tan_send.at[s],
            recv_sem=tan_recv.at[other],
            device_id={"atom": other},
            device_id_type=MESH,
        )

    def force_copy(s):
        other = target(s)
        return pltpu.make_async_remote_copy(
            src_ref=part_all.at[other],
            dst_ref=recv_all.at[me],
            send_sem=force_send.at[s],
            recv_sem=force_recv.at[me],
            device_id={"atom": other},
            device_id_type=MESH,
        )

    def force_arrival(s):
        other = target(s)
        return pltpu.make_async_remote_copy(
            src_ref=part_all.at[other],
            dst_ref=recv_all.at[other],
            send_sem=force_send.at[s],
            recv_sem=force_recv.at[other],
            device_id={"atom": other},
            device_id_type=MESH,
        )

    tile_line = lax.broadcasted_iota(i32, (tile, WIDE), 0)
    greeted = (n_atom - 1) + jnp.where(img > 0, 1, 0) + jnp.where(img < n_img - 1, 1, 0)

    def send_coords():
        to_tile(current_t, lambda c: coords_v[c])
        pl.semaphore_wait(barrier, greeted)
        pl.when(img < n_img - 1)(lambda: to_next().start())
        pl.when(img > 0)(lambda: to_previous().start())

    def send_tangent():
        @pl.when(first)
        def _():
            ends[0].wait()
            to_tile(before_t, lambda c: ends_v[0, c : c + 1])

        @pl.when(last)
        def _():
            ends[1].wait()
            to_tile(after_t, lambda c: ends_v[1, c : c + 1])

        pl.when(img > 0)(lambda: to_next().wait_recv())
        pl.when(img < n_img - 1)(lambda: to_previous().wait_recv())
        current, before, after = current_t[...], before_t[...], after_t[...]
        ahead = jnp.sum((after - current) ** 2, axis=0, keepdims=True)
        behind = jnp.sum((current - before) ** 2, axis=0, keepdims=True)
        mine = after - before
        mine = jnp.where(tile_line == LINES - 1, ahead, mine)
        mine = jnp.where(tile_line == 2 * LINES - 1, behind, mine)
        tan_all[me] = mine
        for s in range(1, n_atom):
            tangent_copy(s).start()

    middle = min(2, n_chunks - 1)
    total[...] = jnp.zeros_like(total)
    total_own[...] = jnp.zeros_like(total_own)
    lax.fori_loop(0, n_chunks, prepare, 0)
    send_coords()
    lax.fori_loop(0, n_chunks, work, 0)

    for s in range(1, n_atom):
        tangent_arrival(s).wait_recv()
    partner_sum = total[:n_rows, :] + total[n_rows:, :]
    own_sum = total_own[:tile, :] + total_own[tile:, :]
    plain = tile_line % LINES < n_comp
    parts, dot = [], jnp.zeros((tile, WIDE), f32)
    square = jnp.zeros((tile, WIDE), f32)
    sums = jnp.zeros((tile, WIDE), f32)
    for d in range(n_atom):
        value = jnp.where(me == d, own_sum, 0.0) - partner_sum[d * tile : (d + 1) * tile]
        other = tan_all[d]
        tangent = jnp.where(plain, other, 0.0)
        dot = dot + value * tangent
        square = square + tangent * tangent
        sums = sums + other
        parts.append(value)
    dot = jnp.sum(dot, axis=0, keepdims=True)
    for d in range(n_atom):
        part_all[d] = jnp.where(tile_line == LINES - 1, dot, parts[d])
    for s in range(1, n_atom):
        force_copy(s).start()
    recv_all[me] = part_all[me]
    length = jnp.sum(square, keepdims=True)
    ahead = jnp.sum(sums[LINES - 1 : LINES], keepdims=True)
    behind = jnp.sum(sums[2 * LINES - 1 : 2 * LINES], keepdims=True)
    inverse = 1.0 / jnp.sqrt(length + tangent_eps)
    spring = spring_const * (jnp.sqrt(ahead) - jnp.sqrt(behind))
    for s in range(1, n_atom):
        force_arrival(s).wait_recv()
    summed = recv_all[0]
    for d in range(1, n_atom):
        summed = summed + recv_all[d]
    along = jnp.sum(summed[LINES - 1 : LINES], keepdims=True) * inverse
    pull = ((spring - along) * inverse) * tan_all[me]
    for h in range(rows_own):
        for c in range(n_comp):
            row = h * LINES + c
            force_out[c, :, h * WIDE : (h + 1) * WIDE] = summed[row : row + 1]
            pull_out[c, :, h * WIDE : (h + 1) * WIDE] = pull[row : row + 1]
    tangent_out[...] = along
    pl.when(img < n_img - 1)(lambda: to_next().wait_send())
    pl.when(img > 0)(lambda: to_previous().wait_send())
    for s in range(1, n_atom):
        tangent_copy(s).wait_send()
        force_copy(s).wait_send()


def solution(mesh):
    n_img, n_atom = mesh.shape["img"], mesh.shape["atom"]

    def local(density, energy, dham, dovl, owner, partner, kind, count, species, *rest):
        orbitals, coords, reactant, product = rest
        dham, dovl = (jnp.transpose(x, (0, 2, 3, 1, 4)) for x in (dham, dovl))
        coords = jnp.transpose(coords, (1, 0, 2))
        args = (density, energy, dham, dovl, owner, partner, kind, count, species)
        args += (orbitals, coords, reactant, product)
        n_slots, n_orb = owner.shape[1], density.shape[1]
        chunk = next(c for c in (512, 256, 128) if n_slots % c == 0)
        tile = species.shape[0] // WIDE * LINES
        tiles = (n_atom, tile, WIDE)
        dma = pltpu.SemaphoreType.DMA
        force, pull, along = pl.pallas_call(
            functools.partial(step_kernel, n_img, n_atom, chunk),
            out_shape=(
                jax.ShapeDtypeStruct(coords.shape, jnp.float32),
                jax.ShapeDtypeStruct(coords.shape, jnp.float32),
                jax.ShapeDtypeStruct((1, 1), jnp.float32),
            ),
            in_specs=[pl.BlockSpec(memory_space=pltpu.HBM)] * len(args),
            out_specs=(
                pl.BlockSpec(memory_space=pltpu.VMEM),
                pl.BlockSpec(memory_space=pltpu.VMEM),
                pl.BlockSpec(memory_space=pltpu.VMEM),
            ),
            scratch_shapes=[
                pltpu.VMEM(density.shape[1:], jnp.bfloat16),
                pltpu.VMEM(density.shape[1:], jnp.bfloat16),
                pltpu.VMEM(dham.shape[1:], jnp.bfloat16),
                pltpu.VMEM(dham.shape[1:], jnp.bfloat16),
                pltpu.VMEM((n_orb * 16, chunk), jnp.float32),
                pltpu.VMEM((n_orb * 16, chunk), jnp.float32),
                pltpu.VMEM((WIDE, n_slots), jnp.bfloat16),
                pltpu.VMEM((WIDE, n_slots), jnp.bfloat16),
                pltpu.VMEM((8, n_slots), jnp.float32),
                pltpu.VMEM((2 * n_atom * tile, WIDE), jnp.float32),
                pltpu.VMEM((2 * tile, WIDE), jnp.float32),
                pltpu.VMEM(owner.shape, jnp.int32),
                pltpu.VMEM(owner.shape, jnp.int32),
                pltpu.VMEM(owner.shape, jnp.int32),
                pltpu.SMEM(count.shape, jnp.int32),
                pltpu.VMEM(species.shape, jnp.int32),
                pltpu.SMEM(orbitals.shape, jnp.int32),
                pltpu.VMEM(coords.shape, jnp.float32),
                pltpu.VMEM((2,) + reactant.shape, jnp.float32),
                pltpu.VMEM(tiles[1:], jnp.float32),
                pltpu.VMEM(tiles[1:], jnp.float32),
                pltpu.VMEM(tiles[1:], jnp.float32),
                pltpu.VMEM(tiles, jnp.float32),
                pltpu.VMEM(tiles, jnp.float32),
                pltpu.VMEM(tiles, jnp.float32),
                dma((n_slots // chunk, 4)),
                dma((9,)),
                dma((2,)),
                dma((2,)),
                dma((n_atom,)),
                dma((n_atom,)),
                dma((n_atom,)),
                dma((n_atom,)),
            ],
            compiler_params=pltpu.CompilerParams(
                collective_id=0, has_side_effects=True, vmem_limit_bytes=63 * 1024 * 1024
            ),
        )(*args)
        return jnp.transpose(force + pull, (1, 0, 2)), jnp.reshape(along, (1,))

    return jax.shard_map(
        local,
        mesh=mesh,
        in_specs=(
            P("img", None, None, "atom"),
            P("img", None, None, "atom"),
            P("img", None, None, None, "atom"),
            P("img", None, None, None, "atom"),
            P("img", "atom"),
            P("img", "atom"),
            P("img", "atom"),
            P("img", "atom"),
            P("atom"),
            P(),
            P("img", None, "atom"),
            P(None, "atom"),
            P(None, "atom"),
        ),
        out_specs=(P("img", None, "atom"), P("img")),
        check_vma=False,
    )
```

```python
import functools

import jax
import jax.numpy as jnp
from jax import lax
from jax.experimental import pallas as pl
from jax.experimental.pallas import tpu as pltpu
from jax.sharding import PartitionSpec as P

MESH = pl.DeviceIdType.MESH
spring_const = 1.0
tangent_eps = 1e-06
WIDE = 256
LINES = 4


def step_kernel(
    n_img,
    n_atom,
    chunk,
    density,
    energy,
    dham,
    dovl,
    owner,
    partner,
    partner_species,
    count,
    species,
    orbitals,
    coords,
    reactant,
    product,
    band_out,
    tangent_out,
    dens_v,
    ener_v,
    dham_v,
    dovl_v,
    dens_f,
    ener_f,
    own_hot,
    part_hot,
    orb_v,
    total,
    total_own,
    owner_v,
    partner_v,
    kind_v,
    count_s,
    species_v,
    orbitals_s,
    coords_v,
    ends_v,
    current_t,
    before_t,
    after_t,
    tan_all,
    part_all,
    near_sums,
    middle_sums,
    far_sums,
    block_sem,
    small_sem,
    img_send,
    img_recv,
    tan_send,
    tan_recv,
    force_send,
    force_recv,
):
    f32, bf16, i32 = jnp.float32, jnp.bfloat16, jnp.int32
    img, me = lax.axis_index("img"), lax.axis_index("atom")
    n_lo = max(f for f in range(1, n_atom + 1) if n_atom % f == 0 and f * f <= n_atom)
    n_hi = n_atom // n_lo
    hi, lo = me // n_lo, lax.rem(me, n_lo)
    n_slots = owner.shape[1]
    n_orb = density.shape[1]
    n_comp = dham.shape[3]
    n_kinds = orbitals.shape[0]
    rows_own = species.shape[0] // WIDE
    tile = rows_own * LINES
    n_chunks = n_slots // chunk

    def near(s):
        other = lax.rem(lo + s, n_lo)
        return other, hi * n_lo + other

    def far(s):
        other = lax.rem(hi + s, n_hi)
        return other, other * n_lo + lo

    smalls = [
        (owner, owner_v),
        (partner, partner_v),
        (partner_species, kind_v),
        (count, count_s),
        (species, species_v),
        (orbitals, orbitals_s),
        (coords, coords_v),
    ]
    small_copies = [
        pltpu.make_async_copy(src, dst, small_sem.at[i]) for i, (src, dst) in enumerate(smalls)
    ]
    for copy in small_copies:
        copy.start()
    ends = (
        pltpu.make_async_copy(reactant, ends_v.at[0], small_sem.at[len(smalls)]),
        pltpu.make_async_copy(product, ends_v.at[1], small_sem.at[len(smalls) + 1]),
    )
    first, last = img == 0, img == n_img - 1
    pl.when(first)(ends[0].start)
    pl.when(last)(ends[1].start)

    def block_pairs(k):
        cols = pl.ds(k * chunk if isinstance(k, int) else pl.multiple_of(k * chunk, chunk), chunk)
        return (
            (density.at[0, :, :, cols], dens_v.at[:, :, cols]),
            (energy.at[0, :, :, cols], ener_v.at[:, :, cols]),
            (dham.at[0, :, :, :, cols], dham_v.at[:, :, :, cols]),
            (dovl.at[0, :, :, :, cols], dovl_v.at[:, :, :, cols]),
        )

    def fetch(k, carry):
        for j, (src, dst) in enumerate(block_pairs(k)):
            pltpu.make_async_copy(src, dst, block_sem.at[k, j]).start()
        return carry

    lax.fori_loop(0, n_chunks, fetch, 0)

    barrier = pltpu.get_barrier_semaphore()
    for s in range(1, n_lo):
        pl.semaphore_signal(barrier, inc=1, device_id={"atom": near(s)[1]}, device_id_type=MESH)
    for s in range(1, n_hi):
        pl.semaphore_signal(barrier, inc=1, device_id={"atom": far(s)[1]}, device_id_type=MESH)

    @pl.when(img > 0)
    def _():
        pl.semaphore_signal(barrier, inc=1, device_id={"img": img - 1}, device_id_type=MESH)

    @pl.when(img < n_img - 1)
    def _():
        pl.semaphore_signal(barrier, inc=1, device_id={"img": img + 1}, device_id_type=MESH)

    for copy in small_copies:
        copy.wait()

    kinds_own = species_v[...].reshape(1, species.shape[0])
    table = jnp.zeros(kinds_own.shape, f32)
    for k in range(n_kinds):
        table = jnp.where(kinds_own == k, orbitals_s[k].astype(f32), table)
    table = jnp.concatenate(
        [table[:, h * WIDE : (h + 1) * WIDE] for h in range(rows_own)]
        + [jnp.zeros((16 - rows_own, WIDE), f32)],
        axis=0,
    ).astype(bf16)
    n_rows = n_atom * tile
    shift = WIDE.bit_length() - 1
    pack = 16
    dims = (((1,), (1,)), ((), ()))
    zero = jnp.zeros((), bf16)
    pack_line = lax.broadcasted_iota(i32, (pack, chunk), 0)
    pack_row = pack_line.astype(f32).astype(bf16)
    atom_row = (pack_line // LINES).astype(f32).astype(bf16)
    own_atom_row = (pack_line % tile // LINES).astype(f32).astype(bf16)
    level = lax.broadcasted_iota(i32, (n_orb, chunk), 0).astype(f32).astype(bf16)

    def columns(k):
        return pl.ds(pl.multiple_of(k * chunk, chunk), chunk)

    def small(values):
        return values.astype(f32).astype(bf16)

    def prepare(k, carry):
        cols = columns(k)
        own = owner_v[:, cols]
        part = partner_v[:, cols]
        kind = kind_v[:, cols]
        for index, hot in ((own, own_hot), (part, part_hot)):
            low = jnp.broadcast_to(small(index & (WIDE - 1)), (pack, chunk))
            for g in range(WIDE // pack):
                match = pack_row == low - jnp.asarray(g * pack, bf16)
                hot[g * pack : (g + 1) * pack, cols] = jnp.where(match, zero + 1, zero)
        own_row = own >> shift
        picked = jnp.dot(table, own_hot[:, cols], preferred_element_type=f32)
        own_orb = jnp.zeros((1, chunk), f32)
        for h in range(rows_own):
            own_orb = jnp.where(own_row == h, picked[h : h + 1], own_orb)
        part_orb = jnp.zeros((1, chunk), f32)
        for j in range(n_kinds):
            part_orb = jnp.where(kind == j, orbitals_s[j].astype(f32), part_orb)
        slot = lax.broadcasted_iota(i32, (1, chunk), 1) + k * chunk
        orb_v[0:1, cols] = jnp.where(slot < count_s[0, 0], own_orb, 0.0)
        orb_v[1:2, cols] = part_orb
        return carry

    def work(k, carry):
        pl.when(k == middle)(send_tangent)
        pl.when(k == late)(pass_tangents)
        cols = columns(k)
        own_orb, part_orb = orb_v[0:1, cols], orb_v[1:2, cols]
        for j, (src, dst) in enumerate(block_pairs(k)):
            pltpu.make_async_copy(src, dst, block_sem.at[k, j]).wait()
        for a in range(n_orb):
            bound = jnp.where(own_orb > a, part_orb, 0.0).astype(bf16)
            mask = level < bound
            row = pl.ds(a * 16, n_orb)
            dens_f[row, :] = jnp.where(mask, dens_v[a, :, cols], zero).astype(f32)
            ener_f[row, :] = jnp.where(mask, ener_v[a, :, cols], zero).astype(f32)
        acc = [jnp.zeros((n_comp, chunk), f32) for _ in range(2)]
        for a in range(n_orb):
            for b in range(n_orb):
                row = pl.ds(a * 16 + b, 1)
                acc[0] = acc[0] + dens_f[row, :] * dham_v[a, b, :, cols].astype(f32)
                acc[1] = acc[1] + ener_f[row, :] * dovl_v[a, b, :, cols].astype(f32)
        force = -2.0 * (acc[0] - acc[1])
        line = lax.broadcasted_iota(i32, (tile, chunk), 0)
        lines = jnp.zeros((tile, chunk), f32)
        for c in range(n_comp):
            lines = jnp.where(line % LINES == c, force[c : c + 1], lines)
        upper = lines.astype(bf16).astype(f32)
        lower = lines - upper
        own_row = jnp.broadcast_to(small(owner_v[:, cols] >> shift), (pack, chunk))
        part_row = jnp.broadcast_to(small(partner_v[:, cols] >> shift), (pack, chunk))
        both = jnp.concatenate([upper, lower], axis=0).astype(bf16)
        lhs_own = jnp.where(own_atom_row == own_row, both, zero)
        twice = [jnp.concatenate([v] * (pack // tile), axis=0).astype(bf16) for v in (upper, lower)]
        uppers, lowers = [], []
        for g in range(n_rows // pack):
            match = atom_row == part_row - jnp.asarray(g * (pack // LINES), bf16)
            uppers.append(jnp.where(match, twice[0], zero))
            lowers.append(jnp.where(match, twice[1], zero))
        lhs = jnp.concatenate(uppers + lowers, axis=0)
        total[...] += lax.dot_general(lhs, part_hot[:, cols], dims, preferred_element_type=f32)
        total_own[...] += lax.dot_general(
            lhs_own, own_hot[:, cols], dims, preferred_element_type=f32
        )
        return carry

    def to_next():
        return pltpu.make_async_remote_copy(
            src_ref=current_t,
            dst_ref=before_t,
            send_sem=img_send.at[0],
            recv_sem=img_recv.at[0],
            device_id={"img": img + 1},
            device_id_type=MESH,
        )

    def to_previous():
        return pltpu.make_async_remote_copy(
            src_ref=current_t,
            dst_ref=after_t,
            send_sem=img_send.at[1],
            recv_sem=img_recv.at[1],
            device_id={"img": img - 1},
            device_id_type=MESH,
        )

    def to_tile(ref, get):
        ref[...] = jnp.zeros_like(ref)
        for h in range(rows_own):
            for c in range(n_comp):
                row = h * LINES + c
                ref[row : row + 1, :] = get(c)[:, h * WIDE : (h + 1) * WIDE]

    def remote(src, dst, send, recv, device):
        return pltpu.make_async_remote_copy(
            src_ref=src,
            dst_ref=dst,
            send_sem=send,
            recv_sem=recv,
            device_id={"atom": device},
            device_id_type=MESH,
        )

    def tan_near(s, slot):
        place = tan_all.at[hi, slot]
        return remote(place, place, tan_send.at[0, s], tan_recv.at[0, slot], near(s)[1])

    def tan_far(s, slot):
        place = tan_all.at[slot]
        return remote(place, place, tan_send.at[1, s], tan_recv.at[1, slot], far(s)[1])

    def force_near(s, slot):
        other, device = near(s)
        return remote(
            part_all.at[:, other],
            near_sums.at[slot],
            force_send.at[0, s],
            force_recv.at[0, slot],
            device,
        )

    def force_far(s, slot):
        other, device = far(s)
        return remote(
            middle_sums.at[other],
            far_sums.at[slot],
            force_send.at[1, s],
            force_recv.at[1, slot],
            device,
        )

    tile_line = lax.broadcasted_iota(i32, (tile, WIDE), 0)
    greeted = (n_lo - 1) + (n_hi - 1) + jnp.where(img > 0, 1, 0) + jnp.where(img < n_img - 1, 1, 0)

    def send_coords():
        to_tile(current_t, lambda c: coords_v[c])
        pl.semaphore_wait(barrier, greeted)
        pl.when(img < n_img - 1)(lambda: to_next().start())
        pl.when(img > 0)(lambda: to_previous().start())

    def send_tangent():
        @pl.when(first)
        def _():
            ends[0].wait()
            to_tile(before_t, lambda c: ends_v[0, c : c + 1])

        @pl.when(last)
        def _():
            ends[1].wait()
            to_tile(after_t, lambda c: ends_v[1, c : c + 1])

        pl.when(img > 0)(lambda: to_next().wait_recv())
        pl.when(img < n_img - 1)(lambda: to_previous().wait_recv())
        current, before, after = current_t[...], before_t[...], after_t[...]
        ahead = jnp.sum((after - current) ** 2, axis=0, keepdims=True)
        behind = jnp.sum((current - before) ** 2, axis=0, keepdims=True)
        mine = after - before
        mine = jnp.where(tile_line == LINES - 1, ahead, mine)
        mine = jnp.where(tile_line == 2 * LINES - 1, behind, mine)
        tan_all[hi, lo] = mine
        for s in range(1, n_lo):
            tan_near(s, lo).start()

    def pass_tangents():
        for s in range(1, n_lo):
            tan_near(s, near(s)[0]).wait_recv()
        for s in range(1, n_hi):
            tan_far(s, hi).start()

    middle, late = min(2, n_chunks - 1), min(4, n_chunks - 1)
    total[...] = jnp.zeros_like(total)
    total_own[...] = jnp.zeros_like(total_own)
    lax.fori_loop(0, n_chunks, prepare, 0)
    send_coords()
    lax.fori_loop(0, n_chunks, work, 0)

    for s in range(1, n_hi):
        tan_far(s, far(s)[0]).wait_recv()
    partner_sum = total[:n_rows, :] + total[n_rows:, :]
    own_sum = total_own[:tile, :] + total_own[tile:, :]
    plain = tile_line % LINES < n_comp
    parts, dot = [], jnp.zeros((tile, WIDE), f32)
    square = jnp.zeros((tile, WIDE), f32)
    sums = jnp.zeros((tile, WIDE), f32)
    for d in range(n_atom):
        value = jnp.where(me == d, own_sum, 0.0) - partner_sum[d * tile : (d + 1) * tile]
        other = tan_all[d // n_lo, d % n_lo]
        tangent = jnp.where(plain, other, 0.0)
        dot = dot + value * tangent
        square = square + tangent * tangent
        sums = sums + other
        parts.append(value)
    dot = jnp.sum(dot, axis=0, keepdims=True)
    for d in range(n_atom):
        part_all[d // n_lo, d % n_lo] = jnp.where(tile_line == LINES - 1, dot, parts[d])
    for s in range(1, n_lo):
        force_near(s, lo).start()
    length = jnp.sum(square, keepdims=True)
    ahead = jnp.sum(sums[LINES - 1 : LINES], keepdims=True)
    behind = jnp.sum(sums[2 * LINES - 1 : 2 * LINES], keepdims=True)
    inverse = 1.0 / jnp.sqrt(length + tangent_eps)
    spring = spring_const * (jnp.sqrt(ahead) - jnp.sqrt(behind))
    mine = part_all[:, lo]
    for s in range(1, n_lo):
        other = near(s)[0]
        force_near(s, other).wait_recv()
        mine = mine + near_sums[other]
    middle_sums[...] = mine
    for s in range(1, n_hi):
        force_far(s, hi).start()
    summed = middle_sums[hi]
    for s in range(1, n_hi):
        other = far(s)[0]
        force_far(s, other).wait_recv()
        summed = summed + far_sums[other]
    along = jnp.sum(summed[LINES - 1 : LINES], keepdims=True) * inverse
    band = summed + ((spring - along) * inverse) * tan_all[hi, lo]
    for h in range(rows_own):
        for c in range(n_comp):
            row = h * LINES + c
            band_out[c, :, h * WIDE : (h + 1) * WIDE] = band[row : row + 1]
    tangent_out[...] = along
    pl.when(img < n_img - 1)(lambda: to_next().wait_send())
    pl.when(img > 0)(lambda: to_previous().wait_send())
    for s in range(1, n_lo):
        tan_near(s, lo).wait_send()
        force_near(s, lo).wait_send()
    for s in range(1, n_hi):
        tan_far(s, hi).wait_send()
        force_far(s, hi).wait_send()


def solution(mesh):
    n_img, n_atom = mesh.shape["img"], mesh.shape["atom"]

    def local(density, energy, dham, dovl, owner, partner, kind, count, species, *rest):
        orbitals, coords, reactant, product = rest
        dham, dovl = (jnp.transpose(x, (0, 2, 3, 1, 4)) for x in (dham, dovl))
        coords = jnp.transpose(coords, (1, 0, 2))
        args = (density, energy, dham, dovl, owner, partner, kind, count, species)
        args += (orbitals, coords, reactant, product)
        n_slots, n_orb = owner.shape[1], density.shape[1]
        chunk = next(c for c in (512, 256, 128) if n_slots % c == 0)
        tile = species.shape[0] // WIDE * LINES
        n_lo = max(f for f in range(1, n_atom + 1) if n_atom % f == 0 and f * f <= n_atom)
        n_hi = n_atom // n_lo
        tiles = (tile, WIDE)
        dma = pltpu.SemaphoreType.DMA
        band, along = pl.pallas_call(
            functools.partial(step_kernel, n_img, n_atom, chunk),
            out_shape=(
                jax.ShapeDtypeStruct(coords.shape, jnp.float32),
                jax.ShapeDtypeStruct((1, 1), jnp.float32),
            ),
            in_specs=[pl.BlockSpec(memory_space=pltpu.HBM)] * len(args),
            out_specs=(
                pl.BlockSpec(memory_space=pltpu.VMEM),
                pl.BlockSpec(memory_space=pltpu.VMEM),
            ),
            scratch_shapes=[
                pltpu.VMEM(density.shape[1:], jnp.bfloat16),
                pltpu.VMEM(density.shape[1:], jnp.bfloat16),
                pltpu.VMEM(dham.shape[1:], jnp.bfloat16),
                pltpu.VMEM(dham.shape[1:], jnp.bfloat16),
                pltpu.VMEM((n_orb * 16, chunk), jnp.float32),
                pltpu.VMEM((n_orb * 16, chunk), jnp.float32),
                pltpu.VMEM((WIDE, n_slots), jnp.bfloat16),
                pltpu.VMEM((WIDE, n_slots), jnp.bfloat16),
                pltpu.VMEM((8, n_slots), jnp.float32),
                pltpu.VMEM((2 * n_atom * tile, WIDE), jnp.float32),
                pltpu.VMEM((2 * tile, WIDE), jnp.float32),
                pltpu.VMEM(owner.shape, jnp.int32),
                pltpu.VMEM(owner.shape, jnp.int32),
                pltpu.VMEM(owner.shape, jnp.int32),
                pltpu.SMEM(count.shape, jnp.int32),
                pltpu.VMEM(species.shape, jnp.int32),
                pltpu.SMEM(orbitals.shape, jnp.int32),
                pltpu.VMEM(coords.shape, jnp.float32),
                pltpu.VMEM((2,) + reactant.shape, jnp.float32),
                pltpu.VMEM(tiles, jnp.float32),
                pltpu.VMEM(tiles, jnp.float32),
                pltpu.VMEM(tiles, jnp.float32),
                pltpu.VMEM((n_hi, n_lo) + tiles, jnp.float32),
                pltpu.VMEM((n_hi, n_lo) + tiles, jnp.float32),
                pltpu.VMEM((n_lo, n_hi) + tiles, jnp.float32),
                pltpu.VMEM((n_hi,) + tiles, jnp.float32),
                pltpu.VMEM((n_hi,) + tiles, jnp.float32),
                dma((n_slots // chunk, 4)),
                dma((9,)),
                dma((2,)),
                dma((2,)),
                dma((2, n_hi)),
                dma((2, n_hi)),
                dma((2, n_hi)),
                dma((2, n_hi)),
            ],
            compiler_params=pltpu.CompilerParams(
                collective_id=0, has_side_effects=True, vmem_limit_bytes=63 * 1024 * 1024
            ),
        )(*args)
        return jnp.transpose(band, (1, 0, 2)), jnp.reshape(along, (1,))

    return jax.shard_map(
        local,
        mesh=mesh,
        in_specs=(
            P("img", None, None, "atom"),
            P("img", None, None, "atom"),
            P("img", None, None, None, "atom"),
            P("img", None, None, None, "atom"),
            P("img", "atom"),
            P("img", "atom"),
            P("img", "atom"),
            P("img", "atom"),
            P("atom"),
            P(),
            P("img", None, "atom"),
            P(None, "atom"),
            P(None, "atom"),
        ),
        out_specs=(P("img", None, "atom"), P("img")),
        check_vma=False,
    )
```

```python
import functools

import jax
import jax.numpy as jnp
from jax import lax
from jax.experimental import pallas as pl
from jax.experimental.pallas import tpu as pltpu
from jax.sharding import PartitionSpec as P

MESH = pl.DeviceIdType.MESH
spring_const = 1.0
tangent_eps = 1e-06
WIDE = 256
LINES = 4


def step_kernel(
    n_img,
    n_atom,
    chunk,
    density,
    energy,
    dham,
    dovl,
    owner,
    partner,
    partner_species,
    count,
    species,
    orbitals,
    coords,
    reactant,
    product,
    band_out,
    tangent_out,
    dens_v,
    ener_v,
    dham_v,
    dovl_v,
    dens_f,
    ener_f,
    own_hot,
    part_hot,
    orb_v,
    total,
    total_own,
    owner_v,
    partner_v,
    kind_v,
    count_s,
    species_v,
    orbitals_s,
    coords_v,
    ends_v,
    current_t,
    before_t,
    after_t,
    tan_all,
    part_all,
    recv_all,
    block_sem,
    small_sem,
    img_send,
    img_recv,
    tan_send,
    tan_recv,
    force_send,
    force_recv,
):
    f32, bf16, i32 = jnp.float32, jnp.bfloat16, jnp.int32
    img, me = lax.axis_index("img"), lax.axis_index("atom")
    n_slots = owner.shape[1]
    n_orb = density.shape[1]
    n_comp = dham.shape[3]
    n_kinds = orbitals.shape[0]
    rows_own = species.shape[0] // WIDE
    tile = rows_own * LINES
    n_chunks = n_slots // chunk

    barrier = pltpu.get_barrier_semaphore()
    for s in range(1, n_atom):
        pl.semaphore_signal(
            barrier, inc=1, device_id={"atom": lax.rem(me + s, n_atom)}, device_id_type=MESH
        )

    @pl.when(img > 0)
    def _():
        pl.semaphore_signal(barrier, inc=1, device_id={"img": img - 1}, device_id_type=MESH)

    @pl.when(img < n_img - 1)
    def _():
        pl.semaphore_signal(barrier, inc=1, device_id={"img": img + 1}, device_id_type=MESH)

    smalls = [
        (coords, coords_v),
        (owner, owner_v),
        (partner, partner_v),
        (partner_species, kind_v),
        (count, count_s),
        (species, species_v),
        (orbitals, orbitals_s),
    ]
    small_copies = [
        pltpu.make_async_copy(src, dst, small_sem.at[i]) for i, (src, dst) in enumerate(smalls)
    ]
    for copy in small_copies:
        copy.start()
    ends = (
        pltpu.make_async_copy(reactant, ends_v.at[0], small_sem.at[len(smalls)]),
        pltpu.make_async_copy(product, ends_v.at[1], small_sem.at[len(smalls) + 1]),
    )
    first, last = img == 0, img == n_img - 1
    pl.when(first)(ends[0].start)
    pl.when(last)(ends[1].start)

    def block_pairs(k):
        cols = pl.ds(k * chunk if isinstance(k, int) else pl.multiple_of(k * chunk, chunk), chunk)
        return (
            (density.at[0, :, :, cols], dens_v.at[:, :, cols]),
            (energy.at[0, :, :, cols], ener_v.at[:, :, cols]),
            (dham.at[0, :, :, :, cols], dham_v.at[:, :, :, cols]),
            (dovl.at[0, :, :, :, cols], dovl_v.at[:, :, :, cols]),
        )

    def fetch(k, carry):
        for j, (src, dst) in enumerate(block_pairs(k)):
            pltpu.make_async_copy(src, dst, block_sem.at[k, j]).start()
        return carry

    lax.fori_loop(0, n_chunks, fetch, 0)

    for copy in small_copies[1:]:
        copy.wait()

    kinds_own = species_v[...].reshape(1, species.shape[0])
    table = jnp.zeros(kinds_own.shape, f32)
    for k in range(n_kinds):
        table = jnp.where(kinds_own == k, orbitals_s[k].astype(f32), table)
    table = jnp.concatenate(
        [table[:, h * WIDE : (h + 1) * WIDE] for h in range(rows_own)]
        + [jnp.zeros((16 - rows_own, WIDE), f32)],
        axis=0,
    ).astype(bf16)
    n_rows = n_atom * tile
    shift = WIDE.bit_length() - 1
    pack = 16
    dims = (((1,), (1,)), ((), ()))
    zero = jnp.zeros((), bf16)
    pack_line = lax.broadcasted_iota(i32, (pack, chunk), 0)
    pack_row = pack_line.astype(f32).astype(bf16)
    atom_row = (pack_line // LINES).astype(f32).astype(bf16)
    own_atom_row = (pack_line % tile // LINES).astype(f32).astype(bf16)
    level = lax.broadcasted_iota(i32, (n_orb, chunk), 0).astype(f32).astype(bf16)

    def columns(k):
        return pl.ds(pl.multiple_of(k * chunk, chunk), chunk)

    def small(values):
        return values.astype(f32).astype(bf16)

    def prepare(k, carry):
        cols = columns(k)
        own = owner_v[:, cols]
        part = partner_v[:, cols]
        kind = kind_v[:, cols]
        for index, hot in ((own, own_hot), (part, part_hot)):
            low = jnp.broadcast_to(small(index & (WIDE - 1)), (pack, chunk))
            for g in range(WIDE // pack):
                match = pack_row == low - jnp.asarray(g * pack, bf16)
                hot[g * pack : (g + 1) * pack, cols] = jnp.where(match, zero + 1, zero)
        own_row = own >> shift
        picked = jnp.dot(table, own_hot[:, cols], preferred_element_type=f32)
        own_orb = jnp.zeros((1, chunk), f32)
        for h in range(rows_own):
            own_orb = jnp.where(own_row == h, picked[h : h + 1], own_orb)
        part_orb = jnp.zeros((1, chunk), f32)
        for j in range(n_kinds):
            part_orb = jnp.where(kind == j, orbitals_s[j].astype(f32), part_orb)
        slot = lax.broadcasted_iota(i32, (1, chunk), 1) + k * chunk
        orb_v[0:1, cols] = jnp.where(slot < count_s[0, 0], own_orb, 0.0)
        orb_v[1:2, cols] = part_orb
        return carry

    def work(k, carry):
        cols = columns(k)
        own_orb, part_orb = orb_v[0:1, cols], orb_v[1:2, cols]
        for j, (src, dst) in enumerate(block_pairs(k)):
            pltpu.make_async_copy(src, dst, block_sem.at[k, j]).wait()
        for a in range(n_orb):
            bound = jnp.where(own_orb > a, part_orb, 0.0).astype(bf16)
            mask = level < bound
            row = pl.ds(a * 16, n_orb)
            dens_f[row, :] = jnp.where(mask, dens_v[a, :, cols], zero).astype(f32)
            ener_f[row, :] = jnp.where(mask, ener_v[a, :, cols], zero).astype(f32)
        acc = [jnp.zeros((n_comp, chunk), f32) for _ in range(2)]
        for a in range(n_orb):
            for b in range(n_orb):
                row = pl.ds(a * 16 + b, 1)
                acc[0] = acc[0] + dens_f[row, :] * dham_v[a, b, :, cols].astype(f32)
                acc[1] = acc[1] + ener_f[row, :] * dovl_v[a, b, :, cols].astype(f32)
        force = -2.0 * (acc[0] - acc[1])
        line = lax.broadcasted_iota(i32, (tile, chunk), 0)
        lines = jnp.zeros((tile, chunk), f32)
        for c in range(n_comp):
            lines = jnp.where(line % LINES == c, force[c : c + 1], lines)
        upper = lines.astype(bf16).astype(f32)
        lower = lines - upper
        own_row = jnp.broadcast_to(small(owner_v[:, cols] >> shift), (pack, chunk))
        part_row = jnp.broadcast_to(small(partner_v[:, cols] >> shift), (pack, chunk))
        both = jnp.concatenate([upper, lower], axis=0).astype(bf16)
        lhs_own = jnp.where(own_atom_row == own_row, both, zero)
        twice = [jnp.concatenate([v] * (pack // tile), axis=0).astype(bf16) for v in (upper, lower)]
        uppers, lowers = [], []
        for g in range(n_rows // pack):
            match = atom_row == part_row - jnp.asarray(g * (pack // LINES), bf16)
            uppers.append(jnp.where(match, twice[0], zero))
            lowers.append(jnp.where(match, twice[1], zero))
        lhs = jnp.concatenate(uppers + lowers, axis=0)
        total[...] += lax.dot_general(lhs, part_hot[:, cols], dims, preferred_element_type=f32)
        total_own[...] += lax.dot_general(
            lhs_own, own_hot[:, cols], dims, preferred_element_type=f32
        )
        return carry

    def to_next():
        return pltpu.make_async_remote_copy(
            src_ref=current_t,
            dst_ref=before_t,
            send_sem=img_send.at[0],
            recv_sem=img_recv.at[0],
            device_id={"img": img + 1},
            device_id_type=MESH,
        )

    def to_previous():
        return pltpu.make_async_remote_copy(
            src_ref=current_t,
            dst_ref=after_t,
            send_sem=img_send.at[1],
            recv_sem=img_recv.at[1],
            device_id={"img": img - 1},
            device_id_type=MESH,
        )

    def to_tile(ref, get):
        ref[...] = jnp.zeros_like(ref)
        for h in range(rows_own):
            for c in range(n_comp):
                row = h * LINES + c
                ref[row : row + 1, :] = get(c)[:, h * WIDE : (h + 1) * WIDE]

    def target(s):
        return lax.rem(me + s, n_atom)

    def tangent_copy(s):
        return pltpu.make_async_remote_copy(
            src_ref=tan_all.at[me],
            dst_ref=tan_all.at[me],
            send_sem=tan_send.at[s],
            recv_sem=tan_recv.at[me],
            device_id={"atom": target(s)},
            device_id_type=MESH,
        )

    def tangent_arrival(s):
        other = target(s)
        return pltpu.make_async_remote_copy(
            src_ref=tan_all.at[other],
            dst_ref=tan_all.at[other],
            send_sem=tan_send.at[s],
            recv_sem=tan_recv.at[other],
            device_id={"atom": other},
            device_id_type=MESH,
        )

    def force_copy(s):
        other = target(s)
        return pltpu.make_async_remote_copy(
            src_ref=part_all.at[other],
            dst_ref=recv_all.at[me],
            send_sem=force_send.at[s],
            recv_sem=force_recv.at[me],
            device_id={"atom": other},
            device_id_type=MESH,
        )

    def force_arrival(s):
        other = target(s)
        return pltpu.make_async_remote_copy(
            src_ref=part_all.at[other],
            dst_ref=recv_all.at[other],
            send_sem=force_send.at[s],
            recv_sem=force_recv.at[other],
            device_id={"atom": other},
            device_id_type=MESH,
        )

    tile_line = lax.broadcasted_iota(i32, (tile, WIDE), 0)
    greeted = (n_atom - 1) + jnp.where(img > 0, 1, 0) + jnp.where(img < n_img - 1, 1, 0)

    def send_coords():
        small_copies[0].wait()
        to_tile(current_t, lambda c: coords_v[c])
        pl.semaphore_wait(barrier, greeted)
        pl.when(img < n_img - 1)(lambda: to_next().start())
        pl.when(img > 0)(lambda: to_previous().start())

    def send_tangent():
        @pl.when(first)
        def _():
            ends[0].wait()
            to_tile(before_t, lambda c: ends_v[0, c : c + 1])

        @pl.when(last)
        def _():
            ends[1].wait()
            to_tile(after_t, lambda c: ends_v[1, c : c + 1])

        pl.when(img > 0)(lambda: to_next().wait_recv())
        pl.when(img < n_img - 1)(lambda: to_previous().wait_recv())
        current, before, after = current_t[...], before_t[...], after_t[...]
        ahead = jnp.sum((after - current) ** 2, axis=0, keepdims=True)
        behind = jnp.sum((current - before) ** 2, axis=0, keepdims=True)
        mine = after - before
        mine = jnp.where(tile_line == LINES - 1, ahead, mine)
        mine = jnp.where(tile_line == 2 * LINES - 1, behind, mine)
        tan_all[me] = mine
        for s in range(1, n_atom):
            tangent_copy(s).start()

    total[...] = jnp.zeros_like(total)
    total_own[...] = jnp.zeros_like(total_own)
    send_coords()
    lax.fori_loop(0, n_chunks, prepare, 0)
    send_tangent()
    lax.fori_loop(0, n_chunks, work, 0)

    for s in range(1, n_atom):
        tangent_arrival(s).wait_recv()
    partner_sum = total[:n_rows, :] + total[n_rows:, :]
    own_sum = total_own[:tile, :] + total_own[tile:, :]
    plain = tile_line % LINES < n_comp
    parts, dot = [], jnp.zeros((tile, WIDE), f32)
    square = jnp.zeros((tile, WIDE), f32)
    sums = jnp.zeros((tile, WIDE), f32)
    for d in range(n_atom):
        value = jnp.where(me == d, own_sum, 0.0) - partner_sum[d * tile : (d + 1) * tile]
        other = tan_all[d]
        tangent = jnp.where(plain, other, 0.0)
        dot = dot + value * tangent
        square = square + tangent * tangent
        sums = sums + other
        parts.append(value)
    dot = jnp.sum(dot, axis=0, keepdims=True)
    for d in range(n_atom):
        part_all[d] = jnp.where(tile_line == LINES - 1, dot, parts[d])
    for s in range(1, n_atom):
        force_copy(s).start()
    recv_all[me] = part_all[me]
    length = jnp.sum(square, keepdims=True)
    ahead = jnp.sum(sums[LINES - 1 : LINES], keepdims=True)
    behind = jnp.sum(sums[2 * LINES - 1 : 2 * LINES], keepdims=True)
    inverse = 1.0 / jnp.sqrt(length + tangent_eps)
    spring = spring_const * (jnp.sqrt(ahead) - jnp.sqrt(behind))
    for s in range(1, n_atom):
        force_arrival(s).wait_recv()
    summed = recv_all[0]
    for d in range(1, n_atom):
        summed = summed + recv_all[d]
    along = jnp.sum(summed[LINES - 1 : LINES], keepdims=True) * inverse
    band = summed + ((spring - along) * inverse) * tan_all[me]
    for h in range(rows_own):
        for c in range(n_comp):
            row = h * LINES + c
            band_out[c, :, h * WIDE : (h + 1) * WIDE] = band[row : row + 1]
    tangent_out[...] = along
    pl.when(img < n_img - 1)(lambda: to_next().wait_send())
    pl.when(img > 0)(lambda: to_previous().wait_send())
    for s in range(1, n_atom):
        tangent_copy(s).wait_send()
        force_copy(s).wait_send()


def solution(mesh):
    n_img, n_atom = mesh.shape["img"], mesh.shape["atom"]

    def local(density, energy, dham, dovl, owner, partner, kind, count, species, *rest):
        orbitals, coords, reactant, product = rest
        dham, dovl = (jnp.transpose(x, (0, 2, 3, 1, 4)) for x in (dham, dovl))
        coords = jnp.transpose(coords, (1, 0, 2))
        args = (density, energy, dham, dovl, owner, partner, kind, count, species)
        args += (orbitals, coords, reactant, product)
        n_slots, n_orb = owner.shape[1], density.shape[1]
        chunk = next(c for c in (512, 256, 128) if n_slots % c == 0)
        tile = species.shape[0] // WIDE * LINES
        tiles = (n_atom, tile, WIDE)
        dma = pltpu.SemaphoreType.DMA
        band, along = pl.pallas_call(
            functools.partial(step_kernel, n_img, n_atom, chunk),
            out_shape=(
                jax.ShapeDtypeStruct(coords.shape, jnp.float32),
                jax.ShapeDtypeStruct((1, 1), jnp.float32),
            ),
            in_specs=[pl.BlockSpec(memory_space=pltpu.HBM)] * len(args),
            out_specs=(
                pl.BlockSpec(memory_space=pltpu.VMEM),
                pl.BlockSpec(memory_space=pltpu.VMEM),
            ),
            scratch_shapes=[
                pltpu.VMEM(density.shape[1:], jnp.bfloat16),
                pltpu.VMEM(density.shape[1:], jnp.bfloat16),
                pltpu.VMEM(dham.shape[1:], jnp.bfloat16),
                pltpu.VMEM(dham.shape[1:], jnp.bfloat16),
                pltpu.VMEM((n_orb * 16, chunk), jnp.float32),
                pltpu.VMEM((n_orb * 16, chunk), jnp.float32),
                pltpu.VMEM((WIDE, n_slots), jnp.bfloat16),
                pltpu.VMEM((WIDE, n_slots), jnp.bfloat16),
                pltpu.VMEM((8, n_slots), jnp.float32),
                pltpu.VMEM((2 * n_atom * tile, WIDE), jnp.float32),
                pltpu.VMEM((2 * tile, WIDE), jnp.float32),
                pltpu.VMEM(owner.shape, jnp.int32),
                pltpu.VMEM(owner.shape, jnp.int32),
                pltpu.VMEM(owner.shape, jnp.int32),
                pltpu.SMEM(count.shape, jnp.int32),
                pltpu.VMEM(species.shape, jnp.int32),
                pltpu.SMEM(orbitals.shape, jnp.int32),
                pltpu.VMEM(coords.shape, jnp.float32),
                pltpu.VMEM((2,) + reactant.shape, jnp.float32),
                pltpu.VMEM(tiles[1:], jnp.float32),
                pltpu.VMEM(tiles[1:], jnp.float32),
                pltpu.VMEM(tiles[1:], jnp.float32),
                pltpu.VMEM(tiles, jnp.float32),
                pltpu.VMEM(tiles, jnp.float32),
                pltpu.VMEM(tiles, jnp.float32),
                dma((n_slots // chunk, 4)),
                dma((9,)),
                dma((2,)),
                dma((2,)),
                dma((n_atom,)),
                dma((n_atom,)),
                dma((n_atom,)),
                dma((n_atom,)),
            ],
            compiler_params=pltpu.CompilerParams(
                collective_id=0, has_side_effects=True, vmem_limit_bytes=63 * 1024 * 1024
            ),
        )(*args)
        return jnp.transpose(band, (1, 0, 2)), jnp.reshape(along, (1,))

    return jax.shard_map(
        local,
        mesh=mesh,
        in_specs=(
            P("img", None, None, "atom"),
            P("img", None, None, "atom"),
            P("img", None, None, None, "atom"),
            P("img", None, None, None, "atom"),
            P("img", "atom"),
            P("img", "atom"),
            P("img", "atom"),
            P("img", "atom"),
            P("atom"),
            P(),
            P("img", None, "atom"),
            P(None, "atom"),
            P(None, "atom"),
        ),
        out_specs=(P("img", None, "atom"), P("img")),
        check_vma=False,
    )
```
